32 devices in a mesh: rep: 16 (over z, x, core), shard: 2 (over y).
Axes of the slice: x: 2, y: 2, z: 4, core: 2. Of those that a mesh axis runs over, the one named last changes fastest.
Arguments:
- tokens: bfloat16 [4096, 1024], P(('rep', 'shard')), may hold values from -6 to 6
- cotangent: bfloat16 [4096, 1024], P(('rep', 'shard')), may hold values from -6 to 6
- segment_ids: int32 [4096], P(('rep', 'shard')), may hold values from -1 to 7, as said below
- flat_weights: float32 [12595200], P('shard')
- first_moment: float32 [12595200], P('shard'), may hold values from -1.2 to 1.2
- second_moment: float32 [12595200], P('shard'), may hold values from 0.5 to 2
Outputs:
- output: bfloat16 [4096, 1024], P(('rep', 'shard'))
- input_grad: bfloat16 [4096, 1024], P(('rep', 'shard'))
- weight_grad: float32 [12595200], P('shard')
- new_weights: float32 [12595200], P('shard')
- new_first: float32 [12595200], P('shard')
- new_second: float32 [12595200], P('shard')
The draws below stay inside these ranges and needn't reach their ends.
Inputs may be any that keep to these rules, and one draw needn't show every extreme that they name: `segment_ids`: within each device's 128 rows the live rows come first, numbered 0, 1, 2 ... by sequence and never falling, followed by padding rows of -1; every sequence and every live span is a multiple of 16 rows, and each device has at least a quarter of its rows live. In every draw some device's rows form a single sequence of 128 rows, and some device has 8 sequences.
All inputs are finite; a program needn't handle non-finite values.
Results may differ from the reference program's by a relative error of at most 0.012.
The reference program's roundings to bfloat16 on the way count: a program that leaves them out, or rounds other values in their place, can miss the bound.
Values may be sent and summed in bfloat16 or wider, within the bound.
A program may use at most 512 MiB of HBM per device.

```python
import math
import jax
import jax.numpy as jnp
from jax import lax

D = 1024
HEADS = 16
HD = 64
FF = 4096
STEP = 3
ROWS_DEV = 128
TOKENS = 4096
NPARAM = 12595200


def draw_flat_weights(key, part):
    width = HEADS * HD
    out_fan = max(width * 4 // ROWS_DEV, 1)
    plan = [(D * width, D ** (-0.5), 0), (D * width, D ** (-0.5), 0), (D * width, D ** (-0.5), 0), (width * D, out_fan ** (-0.5), 0), (D * FF, D ** (-0.5), 0), (FF * D, FF ** (-0.5), 0), (width, 0.5, 0), (width, 0.5, 0), (D, 0.5, 0), (D, 0.4, 1), (D, 0.5, 0), (FF, 0.5, 0), (D, 0.5, 0), (D, 0.4, 1), (D, 0.5, 0)]
    pieces = []
    for number, entry in enumerate(plan):
        amount, spread, is_gain = entry
        sub_key = jax.random.fold_in(key, 100 + number)
        if is_gain == 1:
            pieces.append(1.0 + spread * jax.random.uniform(sub_key, (amount,), jnp.float32, -1.0, 1.0))
        else:
            raw = jnp.clip(jax.random.normal(sub_key, (amount,), jnp.float32), -6.0, 6.0)
            pieces.append(raw * spread)
    return jnp.concatenate(pieces)


def draw_segment_ids(key, part):
    devices_all = TOKENS // ROWS_DEV
    unit_rows = ROWS_DEV // 8
    key_live = jax.random.fold_in(key, 11)
    key_full = jax.random.fold_in(key, 12)
    key_start = jax.random.fold_in(key, 13)
    device_ids = jnp.arange(devices_all, dtype=jnp.int32)
    column = jnp.arange(8, dtype=jnp.int32)[None, :]
    full_dev = jax.random.randint(key_full, (), 0, devices_all)
    many_dev = (full_dev + devices_all // 2) % devices_all
    short_dev = (full_dev + 1) % devices_all
    live_units = jax.random.randint(key_live, (devices_all,), 2, 9)
    live_units = jnp.where(device_ids == full_dev, 8, live_units)
    live_units = jnp.where(device_ids == many_dev, 8, live_units)
    live_units = jnp.where(device_ids == short_dev, 2, live_units)
    starts = jax.random.randint(key_start, (devices_all, 8), 0, 3) == 0
    starts = jnp.logical_or(starts, column == 0)
    starts = jnp.where((device_ids == full_dev)[:, None], column == 0, starts)
    starts = jnp.where((device_ids == many_dev)[:, None], column >= 0, starts)
    seq_number = jnp.cumsum(starts.astype(jnp.int32), axis=1) - 1
    labels = jnp.where(column < live_units[:, None], seq_number, -1)
    return jnp.repeat(labels, unit_rows, axis=1).reshape(-1).astype(jnp.int32)


def level_of(stream_key, shape, shards, smallest, top_value):
    level, own = 1.0, jax.random.fold_in(stream_key, 6)
    for position, parts in shards:
        heights = jnp.exp(jax.random.uniform(jax.random.fold_in(own, position), (parts,), jnp.float32, smallest / len(shards), top_value / len(shards)))
        level = level * jnp.repeat(heights, shape[position] // parts).reshape([-1 if axis == position else 1 for axis in range(len(shape))])
    return level


def noise(key, shape, scale, bound, split=(), held_as=jnp.bfloat16):
    drawn = jax.random.normal(key, shape, jnp.float32) * scale
    if len(split) > 0:
        drawn = level_of(key, shape, split, -0.22, 0.18) * drawn
    return jnp.clip(drawn, min=-bound, max=bound).astype(held_as)


def setup_inputs(seed: int = 0) -> dict:
    splits = jax.random.split(jax.random.key(seed), 7)
    return {
        "tokens": noise(splits[0], (TOKENS, D), 1.0, 6.0, ((0, 32),)),
        "cotangent": noise(splits[1], (TOKENS, D), 1.0, 6.0, ((0, 32),)),
        "segment_ids": draw_segment_ids(jax.random.fold_in(splits[6], 71), 0),
        "flat_weights": draw_flat_weights(jax.random.fold_in(splits[6], 71), 0),
        "first_moment": noise(splits[4], (NPARAM,), 0.2, 1.2, ((0, 2),), jnp.float32),
        "second_moment": jnp.clip(jnp.exp(math.log(2.0) - 1.3862944 * jax.random.uniform(splits[5], (NPARAM,), jnp.float32) ** level_of(splits[5], (NPARAM,), ((0, 2),), -0.2, 0.2)), 0.5, 2.0),
    }


def shapes_list():
    width = HEADS * HD
    return [(D, width), (D, width), (D, width), (width, D), (D, FF), (FF, D), (width,), (width,), (D,), (D,), (D,), (FF,), (D,), (D,), (D,)]

def unpack(flat_vec):
    pieces = []
    offset = 0
    for extent in shapes_list():
        amount = math.prod(extent)
        pieces.append(lax.slice_in_dim(flat_vec, offset, offset + amount).reshape(extent))
        offset = offset + amount
    return pieces

def layer_norm(values, gain, shift):
    center = values - lax.optimization_barrier(jnp.mean(values, axis=1, keepdims=True))
    spread = lax.rsqrt(lax.optimization_barrier(jnp.mean(center * center, axis=1, keepdims=True)) + 1e-05)
    normed = center * spread
    return (normed * gain.astype(jnp.float32) + shift.astype(jnp.float32), normed, spread)

def norm_back(upstream, normed, spread, gain):
    scaled = upstream * gain.astype(jnp.float32)
    inner = scaled - lax.optimization_barrier(jnp.mean(scaled, axis=1, keepdims=True)) - normed * lax.optimization_barrier(jnp.mean(scaled * normed, axis=1, keepdims=True))
    return (spread * inner, lax.optimization_barrier(jnp.sum(upstream * normed, axis=0)), lax.optimization_barrier(jnp.sum(upstream, axis=0)))

def gelu_pair(values):
    cdf_part = 0.5 * (1.0 + lax.erf(values * 0.5 ** 0.5))
    density = jnp.exp(-0.5 * values * values) * (2.0 * math.pi) ** (-0.5)
    return (values * cdf_part, cdf_part + values * density)

def heads_of(matrix):
    return matrix.reshape(matrix.shape[0], HEADS, HD).astype(jnp.float32)

def scores_of(query, keys, allowed):
    raw = jnp.einsum('qhd,khd->hqk', heads_of(query), heads_of(keys)) * HD ** (-0.5)
    return jnp.where(allowed[None, :, :], raw, -1e+30)

def layer_block(tokens, cotangent, segment, params):
    query_weight, key_weight, value_weight, output_weight, inner_weight, outer_weight, query_bias, value_bias, output_bias, first_gain, first_shift, inner_bias, outer_bias, second_gain, second_shift = params
    rows = tokens.shape[0]
    residual = tokens.astype(jnp.float32)
    query = (jnp.dot(tokens, query_weight, preferred_element_type=jnp.float32) + query_bias.astype(jnp.float32)).astype(jnp.bfloat16)
    keys = jnp.dot(tokens, key_weight, preferred_element_type=jnp.float32).astype(jnp.bfloat16)
    values = (jnp.dot(tokens, value_weight, preferred_element_type=jnp.float32) + value_bias.astype(jnp.float32)).astype(jnp.bfloat16)
    allowed = segment[:, None] == segment[None, :]
    scores = scores_of(query, keys, allowed)
    row_max = lax.optimization_barrier(jnp.max(scores, axis=2, keepdims=True))
    expo = jnp.exp(scores - row_max)
    row_sum = lax.optimization_barrier(jnp.sum(expo, axis=2, keepdims=True))
    log_sum = row_max + jnp.log(row_sum)
    attn_prob = (expo / row_sum).astype(jnp.bfloat16)
    context = jnp.einsum('hqk,khd->qhd', attn_prob.astype(jnp.float32), heads_of(values)).reshape(rows, HEADS * HD).astype(jnp.bfloat16)
    attended = jnp.dot(context, output_weight, preferred_element_type=jnp.float32) + output_bias.astype(jnp.float32)
    first_norm, first_normed, first_spread = layer_norm(residual + attended, first_gain, first_shift)
    first_round = first_norm.astype(jnp.bfloat16)
    inner_pre = jnp.dot(first_round, inner_weight, preferred_element_type=jnp.float32) + inner_bias.astype(jnp.float32)
    inner_act, inner_slope = gelu_pair(inner_pre)
    inner_round = inner_act.astype(jnp.bfloat16)
    outer = jnp.dot(inner_round, outer_weight, preferred_element_type=jnp.float32) + outer_bias.astype(jnp.float32)
    second_norm, second_normed, second_spread = layer_norm(first_norm + outer, second_gain, second_shift)
    live = (segment >= 0)[:, None]
    output = jnp.where(live, second_norm, residual).astype(jnp.bfloat16)
    upstream = jnp.where(live, cotangent.astype(jnp.float32), 0.0)
    back_second, grad_second_gain, grad_second_shift = norm_back(upstream, second_normed, second_spread, second_gain)
    back_second_round = back_second.astype(jnp.bfloat16)
    grad_outer_weight = jnp.dot(inner_round.T, back_second_round, preferred_element_type=jnp.float32)
    grad_outer_bias = lax.optimization_barrier(jnp.sum(back_second, axis=0))
    back_inner = jnp.dot(back_second_round, outer_weight.T, preferred_element_type=jnp.float32) * inner_slope
    back_inner_round = back_inner.astype(jnp.bfloat16)
    grad_inner_weight = jnp.dot(first_round.T, back_inner_round, preferred_element_type=jnp.float32)
    grad_inner_bias = lax.optimization_barrier(jnp.sum(back_inner, axis=0))
    back_first_out = back_second + jnp.dot(back_inner_round, inner_weight.T, preferred_element_type=jnp.float32)
    back_first, grad_first_gain, grad_first_shift = norm_back(back_first_out, first_normed, first_spread, first_gain)
    back_first_round = back_first.astype(jnp.bfloat16)
    grad_output_weight = jnp.dot(context.T, back_first_round, preferred_element_type=jnp.float32)
    grad_output_bias = lax.optimization_barrier(jnp.sum(back_first, axis=0))
    back_context = jnp.dot(back_first_round, output_weight.T, preferred_element_type=jnp.float32).astype(jnp.bfloat16)
    prob_again = jnp.exp(scores_of(query, keys, allowed) - log_sum)
    prob_round = prob_again.astype(jnp.bfloat16)
    back_values = jnp.einsum('hqk,qhd->khd', prob_round.astype(jnp.float32), heads_of(back_context)).reshape(rows, HEADS * HD)
    back_prob = jnp.einsum('qhd,khd->hqk', heads_of(back_context), heads_of(values))
    delta_rows = lax.optimization_barrier(jnp.sum(heads_of(back_context) * heads_of(context), axis=2)).T
    back_scores = (prob_again * (back_prob - delta_rows[:, :, None]) * HD ** (-0.5)).astype(jnp.bfloat16)
    back_query = jnp.einsum('hqk,khd->qhd', back_scores.astype(jnp.float32), heads_of(keys)).reshape(rows, HEADS * HD)
    back_keys = jnp.einsum('hqk,qhd->khd', back_scores.astype(jnp.float32), heads_of(query)).reshape(rows, HEADS * HD)
    query_round = back_query.astype(jnp.bfloat16)
    keys_round = back_keys.astype(jnp.bfloat16)
    values_round = back_values.astype(jnp.bfloat16)
    grad_query_weight = jnp.dot(tokens.T, query_round, preferred_element_type=jnp.float32)
    grad_key_weight = jnp.dot(tokens.T, keys_round, preferred_element_type=jnp.float32)
    grad_value_weight = jnp.dot(tokens.T, values_round, preferred_element_type=jnp.float32)
    grad_query_bias = lax.optimization_barrier(jnp.sum(back_query, axis=0))
    grad_value_bias = lax.optimization_barrier(jnp.sum(back_values, axis=0))
    back_input = back_first + jnp.dot(query_round, query_weight.T, preferred_element_type=jnp.float32) + jnp.dot(keys_round, key_weight.T, preferred_element_type=jnp.float32) + jnp.dot(values_round, value_weight.T, preferred_element_type=jnp.float32)
    input_grad = jnp.where(live, back_input, cotangent.astype(jnp.float32)).astype(jnp.bfloat16)
    grad_list = [grad_query_weight, grad_key_weight, grad_value_weight, grad_output_weight, grad_inner_weight, grad_outer_weight, grad_query_bias, grad_value_bias, grad_output_bias, grad_first_gain, grad_first_shift, grad_inner_bias, grad_outer_bias, grad_second_gain, grad_second_shift]
    flat_grad = jnp.concatenate([member.reshape(-1) for member in grad_list]).astype(jnp.bfloat16)
    return (output, input_grad, flat_grad)

def adamw(grad, weights, first, second):
    first_new = 0.9 * first + 0.1 * grad
    second_new = 0.98 * second + 0.02 * grad * grad
    first_hat = first_new / (1.0 - 0.9 ** STEP)
    second_hat = second_new / (1.0 - 0.98 ** STEP)
    weights_new = weights - 0.01 * (first_hat / (jnp.sqrt(second_hat) + 1e-06) + 0.01 * weights)
    return (weights_new, first_new, second_new)

def reference(tokens, cotangent, segment_ids, flat_weights, first_moment, second_moment):
    params = unpack(flat_weights.astype(jnp.bfloat16))
    blocks_count = TOKENS // ROWS_DEV
    blocks = (tokens.reshape(blocks_count, ROWS_DEV, D), cotangent.reshape(blocks_count, ROWS_DEV, D), segment_ids.reshape(blocks_count, ROWS_DEV))

    def visit(total, block):
        out_rows, back_rows, flat_grad = layer_block(block[0], block[1], block[2], params)
        term = lax.optimization_barrier(flat_grad).astype(jnp.float32)
        return (total + term, (out_rows, back_rows))
    total, (outs_all, backs_all) = lax.scan(visit, jnp.zeros((NPARAM,), jnp.float32), blocks)
    new_weights, new_first, new_second = adamw(total, flat_weights, first_moment, second_moment)
    return (outs_all.reshape(TOKENS, D), backs_all.reshape(TOKENS, D), total, new_weights, new_first, new_second)
```

```python
import math

import jax
import jax.numpy as jnp
from jax import lax
from jax.experimental import pallas as pl
from jax.experimental.pallas import tpu as pltpu
from jax.sharding import PartitionSpec as P

D = 1024
HEADS = 16
HD = 64
FF = 4096
STEP = 3


def shapes_list():
    width = HEADS * HD
    return [
        (D, width),
        (D, width),
        (D, width),
        (width, D),
        (D, FF),
        (FF, D),
        (width,),
        (width,),
        (D,),
        (D,),
        (D,),
        (FF,),
        (D,),
        (D,),
        (D,),
    ]


def unpack(flat_vec):
    pieces = []
    offset = 0
    for extent in shapes_list():
        amount = math.prod(extent)
        pieces.append(lax.slice_in_dim(flat_vec, offset, offset + amount).reshape(extent))
        offset = offset + amount
    return pieces


def layer_norm(values, gain, shift):
    center = values - jnp.mean(values, axis=1, keepdims=True)
    spread = lax.rsqrt(jnp.mean(center * center, axis=1, keepdims=True) + 1e-05)
    normed = center * spread
    return (normed * gain.astype(jnp.float32) + shift.astype(jnp.float32), normed, spread)


def norm_back(upstream, normed, spread, gain):
    scaled = upstream * gain.astype(jnp.float32)
    inner = (
        scaled
        - jnp.mean(scaled, axis=1, keepdims=True)
        - normed * jnp.mean(scaled * normed, axis=1, keepdims=True)
    )
    return (spread * inner, jnp.sum(upstream * normed, axis=0), jnp.sum(upstream, axis=0))


def gelu_pair(values):
    cdf_part = 0.5 * (1.0 + lax.erf(values * 0.5**0.5))
    density = jnp.exp(-0.5 * values * values) * (2.0 * math.pi) ** (-0.5)
    return (values * cdf_part, cdf_part + values * density)


def heads_of(matrix):
    return matrix.reshape(matrix.shape[0], HEADS, HD)


def scores_of(query, keys, allowed):
    raw = jnp.einsum(
        "qhd,khd->hqk", heads_of(query), heads_of(keys), preferred_element_type=jnp.float32
    ) * HD ** (-0.5)
    return jnp.where(allowed[None, :, :], raw, -1e30)


def forward_pass(tokens, segment, params):
    (
        query_weight,
        key_weight,
        value_weight,
        output_weight,
        inner_weight,
        outer_weight,
        query_bias,
        value_bias,
        output_bias,
        first_gain,
        first_shift,
        inner_bias,
        outer_bias,
        second_gain,
        second_shift,
    ) = params
    rows = tokens.shape[0]
    residual = tokens.astype(jnp.float32)
    query = (
        jnp.dot(tokens, query_weight, preferred_element_type=jnp.float32)
        + query_bias.astype(jnp.float32)
    ).astype(jnp.bfloat16)
    keys = jnp.dot(tokens, key_weight, preferred_element_type=jnp.float32).astype(jnp.bfloat16)
    values = (
        jnp.dot(tokens, value_weight, preferred_element_type=jnp.float32)
        + value_bias.astype(jnp.float32)
    ).astype(jnp.bfloat16)
    allowed = segment[:, None] == segment[None, :]
    scores = scores_of(query, keys, allowed)
    row_max = jnp.max(scores, axis=2, keepdims=True)
    expo = jnp.exp(scores - row_max)
    row_sum = jnp.sum(expo, axis=2, keepdims=True)
    log_sum = row_max + jnp.log(row_sum)
    attn_prob = (expo / row_sum).astype(jnp.bfloat16)
    context = (
        jnp.einsum("hqk,khd->qhd", attn_prob, heads_of(values), preferred_element_type=jnp.float32)
        .reshape(rows, HEADS * HD)
        .astype(jnp.bfloat16)
    )
    attended = jnp.dot(
        context, output_weight, preferred_element_type=jnp.float32
    ) + output_bias.astype(jnp.float32)
    first_norm, first_normed, first_spread = layer_norm(
        residual + attended, first_gain, first_shift
    )
    first_round = first_norm.astype(jnp.bfloat16)
    inner_pre = jnp.dot(
        first_round, inner_weight, preferred_element_type=jnp.float32
    ) + inner_bias.astype(jnp.float32)
    inner_act, inner_slope = gelu_pair(inner_pre)
    inner_round = inner_act.astype(jnp.bfloat16)
    outer = jnp.dot(
        inner_round, outer_weight, preferred_element_type=jnp.float32
    ) + outer_bias.astype(jnp.float32)
    second_norm, second_normed, second_spread = layer_norm(
        first_norm + outer, second_gain, second_shift
    )
    live = (segment >= 0)[:, None]
    output = jnp.where(live, second_norm, residual).astype(jnp.bfloat16)
    saved = (
        query,
        keys,
        values,
        allowed,
        log_sum,
        context,
        first_normed,
        first_spread,
        first_round,
        inner_slope,
        inner_round,
        second_normed,
        second_spread,
        live,
    )
    return (output, saved)


def backward_pass(tokens, cotangent, saved, params):
    (
        query_weight,
        key_weight,
        value_weight,
        output_weight,
        inner_weight,
        outer_weight,
        query_bias,
        value_bias,
        output_bias,
        first_gain,
        first_shift,
        inner_bias,
        outer_bias,
        second_gain,
        second_shift,
    ) = params
    (
        query,
        keys,
        values,
        allowed,
        log_sum,
        context,
        first_normed,
        first_spread,
        first_round,
        inner_slope,
        inner_round,
        second_normed,
        second_spread,
        live,
    ) = saved
    rows = tokens.shape[0]
    upstream = jnp.where(live, cotangent.astype(jnp.float32), 0.0)
    back_second, grad_second_gain, grad_second_shift = norm_back(
        upstream, second_normed, second_spread, second_gain
    )
    back_second_round = back_second.astype(jnp.bfloat16)
    grad_outer_weight = jnp.dot(
        inner_round.T, back_second_round, preferred_element_type=jnp.float32
    )
    grad_outer_bias = jnp.sum(back_second, axis=0)
    back_inner = (
        jnp.dot(back_second_round, outer_weight.T, preferred_element_type=jnp.float32) * inner_slope
    )
    back_inner_round = back_inner.astype(jnp.bfloat16)
    grad_inner_weight = jnp.dot(first_round.T, back_inner_round, preferred_element_type=jnp.float32)
    grad_inner_bias = jnp.sum(back_inner, axis=0)
    back_first_out = back_second + jnp.dot(
        back_inner_round, inner_weight.T, preferred_element_type=jnp.float32
    )
    back_first, grad_first_gain, grad_first_shift = norm_back(
        back_first_out, first_normed, first_spread, first_gain
    )
    back_first_round = back_first.astype(jnp.bfloat16)
    grad_output_weight = jnp.dot(context.T, back_first_round, preferred_element_type=jnp.float32)
    grad_output_bias = jnp.sum(back_first, axis=0)
    back_context = jnp.dot(
        back_first_round, output_weight.T, preferred_element_type=jnp.float32
    ).astype(jnp.bfloat16)
    prob_again = jnp.exp(scores_of(query, keys, allowed) - log_sum)
    prob_round = prob_again.astype(jnp.bfloat16)
    back_values = jnp.einsum(
        "hqk,qhd->khd", prob_round, heads_of(back_context), preferred_element_type=jnp.float32
    ).reshape(rows, HEADS * HD)
    back_prob = jnp.einsum(
        "qhd,khd->hqk", heads_of(back_context), heads_of(values), preferred_element_type=jnp.float32
    )
    delta_rows = jnp.sum(
        heads_of(back_context).astype(jnp.float32) * heads_of(context).astype(jnp.float32), axis=2
    ).T
    back_scores = (prob_again * (back_prob - delta_rows[:, :, None]) * HD ** (-0.5)).astype(
        jnp.bfloat16
    )
    back_query = jnp.einsum(
        "hqk,khd->qhd", back_scores, heads_of(keys), preferred_element_type=jnp.float32
    ).reshape(rows, HEADS * HD)
    back_keys = jnp.einsum(
        "hqk,qhd->khd", back_scores, heads_of(query), preferred_element_type=jnp.float32
    ).reshape(rows, HEADS * HD)
    query_round = back_query.astype(jnp.bfloat16)
    keys_round = back_keys.astype(jnp.bfloat16)
    values_round = back_values.astype(jnp.bfloat16)
    grad_query_weight = jnp.dot(tokens.T, query_round, preferred_element_type=jnp.float32)
    grad_key_weight = jnp.dot(tokens.T, keys_round, preferred_element_type=jnp.float32)
    grad_value_weight = jnp.dot(tokens.T, values_round, preferred_element_type=jnp.float32)
    grad_query_bias = jnp.sum(back_query, axis=0)
    grad_value_bias = jnp.sum(back_values, axis=0)
    back_input = (
        back_first
        + jnp.dot(query_round, query_weight.T, preferred_element_type=jnp.float32)
        + jnp.dot(keys_round, key_weight.T, preferred_element_type=jnp.float32)
        + jnp.dot(values_round, value_weight.T, preferred_element_type=jnp.float32)
    )
    input_grad = jnp.where(live, back_input, cotangent.astype(jnp.float32)).astype(jnp.bfloat16)
    grad_list = [
        grad_query_weight,
        grad_key_weight,
        grad_value_weight,
        grad_output_weight,
        grad_inner_weight,
        grad_outer_weight,
        grad_query_bias,
        grad_value_bias,
        grad_output_bias,
        grad_first_gain,
        grad_first_shift,
        grad_inner_bias,
        grad_outer_bias,
        grad_second_gain,
        grad_second_shift,
    ]
    return (input_grad, grad_list)


def adamw(grad, weights, first, second):
    first_new = 0.9 * first + 0.1 * grad
    second_new = 0.98 * second + 0.02 * grad * grad
    first_hat = first_new / (1.0 - 0.9**STEP)
    second_hat = second_new / (1.0 - 0.98**STEP)
    weights_new = weights - 0.01 * (first_hat / (jnp.sqrt(second_hat) + 1e-06) + 0.01 * weights)
    return (weights_new, first_new, second_new)


def on_device(tokens, cotangent, segment_ids, flat_weights, first_moment, second_moment):
    gathered = lax.all_gather(flat_weights.astype(jnp.bfloat16), "shard", axis=0, tiled=True)
    params = unpack(gathered)
    output, saved = forward_pass(tokens, segment_ids, params)
    input_grad, grads = backward_pass(tokens, cotangent, saved, params)
    local_grad = jnp.concatenate([member.reshape(-1).astype(jnp.bfloat16) for member in grads])
    shards = lax.axis_size("shard")
    owned_len = local_grad.shape[0] // shards
    received = lax.all_to_all(
        local_grad.reshape(shards, owned_len), "shard", split_axis=0, concat_axis=0, tiled=True
    )
    group_part = jnp.sum(received.astype(jnp.float32), axis=0)
    weight_grad = lax.psum(group_part, "rep")
    new_weights, new_first, new_second = adamw(
        weight_grad, flat_weights, first_moment, second_moment
    )
    return (output, input_grad, weight_grad, new_weights, new_first, new_second)


def flip(axis, bit):
    here = lax.axis_index(axis)
    return here + bit * (1 - 2 * (lax.rem(here // bit, 2)))


def own_bit(axis, bit):
    return lax.rem(lax.axis_index(axis) // bit, 2)


LINKS = {
    "core": ("rep", 1),
    "x": ("rep", 2),
    "z1": ("rep", 4),
    "z2": ("rep", 8),
    "y": ("shard", 1),
}


def partner(name):
    axis, bit = LINKS[name]
    return {axis: flip(axis, bit)}


def side(name):
    return own_bit(*LINKS[name])


def greet(names):
    barrier = pltpu.get_barrier_semaphore()
    for name in names:
        pl.semaphore_signal(
            barrier, inc=1, device_id=partner(name), device_id_type=pl.DeviceIdType.MESH
        )
    pl.semaphore_wait(barrier, len(names))


def send(source, target, send_sem, recv_sem, name):
    copy = pltpu.make_async_remote_copy(
        src_ref=source,
        dst_ref=target,
        send_sem=send_sem,
        recv_sem=recv_sem,
        device_id=partner(name),
        device_id_type=pl.DeviceIdType.MESH,
    )
    copy.start()
    return copy


CHUNKS = 6


def gather_kernel(own_ref, full_ref, send_sem, recv_sem, local_sem):
    mine = side("y")
    other = 1 - mine
    quarter = side("x") * 2 + side("core")
    across = (1 - side("x")) * 2 + side("core")
    local = pltpu.make_async_copy(own_ref, full_ref.at[mine], local_sem)
    greet(("y", "x", "core"))
    first = []
    for k in range(CHUNKS):
        first.append(
            send(
                own_ref.at[quarter, k],
                full_ref.at[mine, quarter, k],
                send_sem.at[0, k],
                recv_sem.at[0, k],
                "y",
            )
        )
    local.start()
    second, third, fourth = [], [], []
    for k in range(CHUNKS):
        first[k].wait_recv()
        block = full_ref.at[other, quarter, k]
        second.append(send(block, block, send_sem.at[1, k], recv_sem.at[1, k], "x"))
        third.append(send(block, block, send_sem.at[2, k], recv_sem.at[2, k], "core"))
        if k > 0:
            second[k - 1].wait_recv()
            block = full_ref.at[other, across, k - 1]
            fourth.append(
                send(block, block, send_sem.at[3, k - 1], recv_sem.at[3, k - 1], "core")
            )
    last = CHUNKS - 1
    second[last].wait_recv()
    block = full_ref.at[other, across, last]
    fourth.append(send(block, block, send_sem.at[3, last], recv_sem.at[3, last], "core"))
    for k in range(CHUNKS):
        third[k].wait_recv()
        fourth[k].wait_recv()
        first[k].wait_send()
        second[k].wait_send()
        third[k].wait_send()
        fourth[k].wait_send()
    local.wait()


def gather_params(own):
    rows = own.shape[0]
    chunk = -(-rows // (4 * CHUNKS * 16)) * 16
    padded = jnp.pad(own, ((0, 4 * CHUNKS * chunk - rows), (0, 0)))
    full = pl.pallas_call(
        gather_kernel,
        out_shape=jax.ShapeDtypeStruct((2, 4, CHUNKS, chunk, 128), jnp.bfloat16),
        in_specs=[pl.BlockSpec(memory_space=pl.ANY)],
        out_specs=pl.BlockSpec(memory_space=pl.ANY),
        scratch_shapes=[
            pltpu.SemaphoreType.DMA((4, CHUNKS)),
            pltpu.SemaphoreType.DMA((4, CHUNKS)),
            pltpu.SemaphoreType.DMA,
        ],
        compiler_params=pltpu.CompilerParams(collective_id=0, has_side_effects=True),
        name="gather_params",
    )(padded.reshape(4, CHUNKS, chunk, 128))
    return full.reshape(2, 4 * CHUNKS * chunk, 128)


PLACE = (("x", "z1", "z2"), ("x", "z1", "z2"), ("z1", "x", "z2"))
ORDER = (("y", "x", "z1", "z2"), ("x", "z1", "y", "z2"), ("z1", "y", "x", "z2"))
SUM_LINKS = ("core", "y", "x", "z1", "z2")


def index_of(done, part, name=None, swap=False):
    entries = []
    for dim in ("y",) + PLACE[part]:
        if dim == name:
            entries.append(1 - side(dim) if swap else side(dim))
        elif dim in done:
            entries.append(side(dim))
        else:
            entries.append(slice(None))
    return tuple(entries)


def add_blocks(shape, store, other):
    total = math.prod(shape)

    def body(i, carry):
        index = []
        rest = i
        for extent in reversed(shape):
            index.append(lax.rem(rest, extent))
            rest = rest // extent
        index = tuple(reversed(index))
        here = store.at[index]
        there = other.at[index]
        here[...] = (here[...].astype(jnp.float32) + there[...].astype(jnp.float32)).astype(
            jnp.bfloat16
        )
        return carry

    lax.fori_loop(0, total, body, 0)


def reduce_kernel(grad_ref, out_ref, own, *rest):
    steps = len(ORDER[0])
    landing = [rest[0:3]] + [rest[3 + 3 * t : 6 + 3 * t] for t in range(steps)]
    send_sem, recv_sem, local_sem = rest[3 + 3 * steps :]
    core = side("core")
    greet(SUM_LINKS)
    copies, local = [], []
    for part in range(3):
        copies.append(
            send(
                grad_ref.at[:, part, 1 - core],
                landing[0][part],
                send_sem.at[0, part],
                recv_sem.at[0, part],
                "core",
            )
        )
        own_copy = pltpu.make_async_copy(
            grad_ref.at[:, part, core], own.at[part], local_sem.at[part]
        )
        own_copy.start()
        local.append(own_copy)
    started = list(copies)
    done = [(), (), ()]
    last = [None, None, None]
    for step in range(steps + 1):
        for part in range(3):
            copies[part].wait_recv()
            if step == 0:
                local[part].wait()
                store = own.at[part]
            else:
                name = ORDER[part][step - 1]
                store = own.at[(part,) + index_of(done[part], part, name)]
                done[part] = done[part] + (name,)
            source = landing[step][part]
            lead = source.shape[:-2]
            add_blocks(lead, store, source)
            if step < steps:
                name = ORDER[part][step]
                copies[part] = send(
                    own.at[(part,) + index_of(done[part], part, name, True)],
                    landing[step + 1][part],
                    send_sem.at[step + 1, part],
                    recv_sem.at[step + 1, part],
                    name,
                )
                started.append(copies[part])
            else:
                out_ref[part] = own[(part,) + index_of(done[part], part)]
    for copy in started:
        copy.wait_send()


def reduce_scatter(rows):
    piece, width = rows.shape[0] // 96, rows.shape[1]
    scratch = [pltpu.VMEM((3, 2, 2, 2, 2, piece, width), jnp.bfloat16)]
    scratch += [pltpu.VMEM((2, 2, 2, 2, piece, width), jnp.bfloat16)] * 3
    for step in range(4):
        for part in range(3):
            used = ORDER[part][: step + 1]
            lead = tuple(2 for dim in ("y",) + PLACE[part] if dim not in used)
            scratch.append(pltpu.VMEM(lead + (piece, width), jnp.bfloat16))
    scratch += [
        pltpu.SemaphoreType.DMA((5, 3)),
        pltpu.SemaphoreType.DMA((5, 3)),
        pltpu.SemaphoreType.DMA((3,)),
    ]
    return pl.pallas_call(
        reduce_kernel,
        out_shape=jax.ShapeDtypeStruct((3, piece, width), jnp.bfloat16),
        in_specs=[pl.BlockSpec(memory_space=pl.ANY)],
        out_specs=pl.BlockSpec(memory_space=pltpu.VMEM),
        scratch_shapes=scratch,
        compiler_params=pltpu.CompilerParams(
            collective_id=1, has_side_effects=True, vmem_limit_bytes=56 * 2**20
        ),
        name="reduce_scatter",
    )(rows.reshape(2, 3, 2, 2, 2, 2, piece, width))


SPREAD = (("z2", "z1", "x", "core"), ("z2", "x", "z1", "core"), ("x", "z2", "z1", "core"))


def spread_kernel(piece_ref, full_ref, send_sem, recv_sem, local_sem):
    def index(part, done):
        return (part,) + tuple(
            slice(None) if dim in done else side(dim) for dim in ("core",) + PLACE[part]
        )

    greet(("core", "x", "z1", "z2"))
    copies, local, started = [], [], []
    for part in range(3):
        own_copy = pltpu.make_async_copy(
            piece_ref.at[part], full_ref.at[index(part, ())], local_sem.at[part]
        )
        own_copy.start()
        local.append(own_copy)
    for part in range(3):
        local[part].wait()
    for step in range(4):
        for part in range(3):
            if step > 0:
                copies[part].wait_recv()
            block = full_ref.at[index(part, SPREAD[part][:step])]
            copy = send(
                block,
                block,
                send_sem.at[step, part],
                recv_sem.at[step, part],
                SPREAD[part][step],
            )
            started.append(copy)
            if step > 0:
                copies[part] = copy
            else:
                copies.append(copy)
    for part in range(3):
        copies[part].wait_recv()
    for copy in started:
        copy.wait_send()


def spread(pieces):
    rows = pieces.shape[1]
    full = pl.pallas_call(
        spread_kernel,
        out_shape=jax.ShapeDtypeStruct((3, 2, 2, 2, 2, rows, 128), jnp.bfloat16),
        in_specs=[pl.BlockSpec(memory_space=pl.ANY)],
        out_specs=pl.BlockSpec(memory_space=pl.ANY),
        scratch_shapes=[
            pltpu.SemaphoreType.DMA((4, 3)),
            pltpu.SemaphoreType.DMA((4, 3)),
            pltpu.SemaphoreType.DMA((3,)),
        ],
        compiler_params=pltpu.CompilerParams(collective_id=2, has_side_effects=True),
        name="spread",
    )(pieces)
    return full.reshape(3 * 16 * rows, 128)


def unpack_pair(full, owned_rows):
    pieces = []
    offset = 0
    for extent in shapes_list():
        amount = math.prod(extent) // 128
        members = []
        for shard in range(2):
            low = max(offset - shard * owned_rows, 0)
            high = min(offset + amount - shard * owned_rows, owned_rows)
            if high > low:
                members.append(full[shard, low:high])
        member = members[0] if len(members) == 1 else jnp.concatenate(members)
        pieces.append(member.reshape(extent))
        offset = offset + amount
    return pieces


def on_device_pair(tokens, cotangent, segment_ids, flat_weights, first_moment, second_moment):
    owned = flat_weights.shape[0]
    full = gather_params(flat_weights.reshape(owned // 128, 128).astype(jnp.bfloat16))
    params = unpack_pair(full, owned // 128)
    output, saved = forward_pass(tokens, segment_ids, params)
    input_grad, grads = backward_pass(tokens, cotangent, saved, params)
    rounded = [member.astype(jnp.bfloat16) for member in grads]
    rows = jnp.concatenate([member.reshape(-1, D) for member in rounded[:6]])
    half = rows.shape[0] // 2
    vectors = jnp.concatenate(rounded[6:])
    over = owned - half * D
    tail = jnp.concatenate([rows[half : half + over // D].reshape(-1), vectors])
    tail = lax.optimization_barrier(lax.psum(tail.astype(jnp.float32), ("rep", "shard")))
    pieces = reduce_scatter(rows)
    main = spread(pieces.reshape(3, -1, 128))
    first_shard = lax.axis_index("shard") == 0
    fill = jnp.zeros((vectors.shape[0] - over,), jnp.float32)
    tail = jnp.where(first_shard, jnp.concatenate([tail[:over], fill]), tail[over:])
    joined = jnp.concatenate([main, tail.astype(jnp.bfloat16).reshape(-1, 128)])
    start = jnp.where(first_shard, 0, over // 128)
    weight_grad = lax.dynamic_slice_in_dim(joined, start, owned // 128).astype(jnp.float32)
    weight_grad = weight_grad.reshape(owned)
    new_weights, new_first, new_second = adamw(
        weight_grad, flat_weights, first_moment, second_moment
    )
    return (output, input_grad, weight_grad, new_weights, new_first, new_second)


def solution(mesh):
    paired = mesh.shape["shard"] == 2 and mesh.shape["rep"] == 16
    return jax.shard_map(
        on_device_pair if paired else on_device,
        mesh=mesh,
        in_specs=(
            P(("rep", "shard"), None),
            P(("rep", "shard"), None),
            P(("rep", "shard")),
            P("shard"),
            P("shard"),
            P("shard"),
        ),
        out_specs=(
            P(("rep", "shard"), None),
            P(("rep", "shard"), None),
            P("shard"),
            P("shard"),
            P("shard"),
            P("shard"),
        ),
        check_vma=False,
    )
```

```python
import math

import jax
import jax.numpy as jnp
from jax import lax
from jax.experimental import pallas as pl
from jax.experimental.pallas import tpu as pltpu
from jax.sharding import PartitionSpec as P

D = 1024
HEADS = 16
HD = 64
FF = 4096
STEP = 3


def shapes_list():
    width = HEADS * HD
    return [
        (D, width),
        (D, width),
        (D, width),
        (width, D),
        (D, FF),
        (FF, D),
        (width,),
        (width,),
        (D,),
        (D,),
        (D,),
        (FF,),
        (D,),
        (D,),
        (D,),
    ]


def unpack(flat_vec):
    pieces = []
    offset = 0
    for extent in shapes_list():
        amount = math.prod(extent)
        pieces.append(lax.slice_in_dim(flat_vec, offset, offset + amount).reshape(extent))
        offset = offset + amount
    return pieces


def layer_norm(values, gain, shift):
    center = values - jnp.mean(values, axis=1, keepdims=True)
    spread = lax.rsqrt(jnp.mean(center * center, axis=1, keepdims=True) + 1e-05)
    normed = center * spread
    return (normed * gain.astype(jnp.float32) + shift.astype(jnp.float32), normed, spread)


def norm_back(upstream, normed, spread, gain):
    scaled = upstream * gain.astype(jnp.float32)
    inner = (
        scaled
        - jnp.mean(scaled, axis=1, keepdims=True)
        - normed * jnp.mean(scaled * normed, axis=1, keepdims=True)
    )
    return (spread * inner, jnp.sum(upstream * normed, axis=0), jnp.sum(upstream, axis=0))


def gelu_pair(values):
    cdf_part = 0.5 * (1.0 + lax.erf(values * 0.5**0.5))
    density = jnp.exp(-0.5 * values * values) * (2.0 * math.pi) ** (-0.5)
    return (values * cdf_part, cdf_part + values * density)


def heads_of(matrix):
    return matrix.reshape(matrix.shape[0], HEADS, HD)


def scores_of(query, keys, allowed):
    raw = jnp.einsum(
        "qhd,khd->hqk", heads_of(query), heads_of(keys), preferred_element_type=jnp.float32
    ) * HD ** (-0.5)
    return jnp.where(allowed[None, :, :], raw, -1e30)


def forward_pass(tokens, segment, params):
    (
        query_weight,
        key_weight,
        value_weight,
        output_weight,
        inner_weight,
        outer_weight,
        query_bias,
        value_bias,
        output_bias,
        first_gain,
        first_shift,
        inner_bias,
        outer_bias,
        second_gain,
        second_shift,
    ) = params
    rows = tokens.shape[0]
    residual = tokens.astype(jnp.float32)
    query = (
        jnp.dot(tokens, query_weight, preferred_element_type=jnp.float32)
        + query_bias.astype(jnp.float32)
    ).astype(jnp.bfloat16)
    keys = jnp.dot(tokens, key_weight, preferred_element_type=jnp.float32).astype(jnp.bfloat16)
    values = (
        jnp.dot(tokens, value_weight, preferred_element_type=jnp.float32)
        + value_bias.astype(jnp.float32)
    ).astype(jnp.bfloat16)
    allowed = segment[:, None] == segment[None, :]
    scores = scores_of(query, keys, allowed)
    row_max = jnp.max(scores, axis=2, keepdims=True)
    expo = jnp.exp(scores - row_max)
    row_sum = jnp.sum(expo, axis=2, keepdims=True)
    log_sum = row_max + jnp.log(row_sum)
    attn_prob = (expo / row_sum).astype(jnp.bfloat16)
    context = (
        jnp.einsum("hqk,khd->qhd", attn_prob, heads_of(values), preferred_element_type=jnp.float32)
        .reshape(rows, HEADS * HD)
        .astype(jnp.bfloat16)
    )
    attended = jnp.dot(
        context, output_weight, preferred_element_type=jnp.float32
    ) + output_bias.astype(jnp.float32)
    first_norm, first_normed, first_spread = layer_norm(
        residual + attended, first_gain, first_shift
    )
    first_round = first_norm.astype(jnp.bfloat16)
    inner_pre = jnp.dot(
        first_round, inner_weight, preferred_element_type=jnp.float32
    ) + inner_bias.astype(jnp.float32)
    inner_act, inner_slope = gelu_pair(inner_pre)
    inner_round = inner_act.astype(jnp.bfloat16)
    outer = jnp.dot(
        inner_round, outer_weight, preferred_element_type=jnp.float32
    ) + outer_bias.astype(jnp.float32)
    second_norm, second_normed, second_spread = layer_norm(
        first_norm + outer, second_gain, second_shift
    )
    live = (segment >= 0)[:, None]
    output = jnp.where(live, second_norm, residual).astype(jnp.bfloat16)
    saved = (
        query,
        keys,
        values,
        allowed,
        log_sum,
        context,
        first_normed,
        first_spread,
        first_round,
        inner_slope,
        inner_round,
        second_normed,
        second_spread,
        live,
    )
    return (output, saved)


def backward_pass(tokens, cotangent, saved, params):
    (
        query_weight,
        key_weight,
        value_weight,
        output_weight,
        inner_weight,
        outer_weight,
        query_bias,
        value_bias,
        output_bias,
        first_gain,
        first_shift,
        inner_bias,
        outer_bias,
        second_gain,
        second_shift,
    ) = params
    (
        query,
        keys,
        values,
        allowed,
        log_sum,
        context,
        first_normed,
        first_spread,
        first_round,
        inner_slope,
        inner_round,
        second_normed,
        second_spread,
        live,
    ) = saved
    rows = tokens.shape[0]
    upstream = jnp.where(live, cotangent.astype(jnp.float32), 0.0)
    back_second, grad_second_gain, grad_second_shift = norm_back(
        upstream, second_normed, second_spread, second_gain
    )
    back_second_round = back_second.astype(jnp.bfloat16)
    grad_outer_weight = jnp.dot(
        inner_round.T, back_second_round, preferred_element_type=jnp.float32
    )
    grad_outer_bias = jnp.sum(back_second, axis=0)
    back_inner = (
        jnp.dot(back_second_round, outer_weight.T, preferred_element_type=jnp.float32) * inner_slope
    )
    back_inner_round = back_inner.astype(jnp.bfloat16)
    grad_inner_weight = jnp.dot(first_round.T, back_inner_round, preferred_element_type=jnp.float32)
    grad_inner_bias = jnp.sum(back_inner, axis=0)
    back_first_out = back_second + jnp.dot(
        back_inner_round, inner_weight.T, preferred_element_type=jnp.float32
    )
    back_first, grad_first_gain, grad_first_shift = norm_back(
        back_first_out, first_normed, first_spread, first_gain
    )
    back_first_round = back_first.astype(jnp.bfloat16)
    grad_output_weight = jnp.dot(context.T, back_first_round, preferred_element_type=jnp.float32)
    grad_output_bias = jnp.sum(back_first, axis=0)
    back_context = jnp.dot(
        back_first_round, output_weight.T, preferred_element_type=jnp.float32
    ).astype(jnp.bfloat16)
    prob_again = jnp.exp(scores_of(query, keys, allowed) - log_sum)
    prob_round = prob_again.astype(jnp.bfloat16)
    back_values = jnp.einsum(
        "hqk,qhd->khd", prob_round, heads_of(back_context), preferred_element_type=jnp.float32
    ).reshape(rows, HEADS * HD)
    back_prob = jnp.einsum(
        "qhd,khd->hqk", heads_of(back_context), heads_of(values), preferred_element_type=jnp.float32
    )
    delta_rows = jnp.sum(
        heads_of(back_context).astype(jnp.float32) * heads_of(context).astype(jnp.float32), axis=2
    ).T
    back_scores = (prob_again * (back_prob - delta_rows[:, :, None]) * HD ** (-0.5)).astype(
        jnp.bfloat16
    )
    back_query = jnp.einsum(
        "hqk,khd->qhd", back_scores, heads_of(keys), preferred_element_type=jnp.float32
    ).reshape(rows, HEADS * HD)
    back_keys = jnp.einsum(
        "hqk,qhd->khd", back_scores, heads_of(query), preferred_element_type=jnp.float32
    ).reshape(rows, HEADS * HD)
    query_round = back_query.astype(jnp.bfloat16)
    keys_round = back_keys.astype(jnp.bfloat16)
    values_round = back_values.astype(jnp.bfloat16)
    grad_query_weight = jnp.dot(tokens.T, query_round, preferred_element_type=jnp.float32)
    grad_key_weight = jnp.dot(tokens.T, keys_round, preferred_element_type=jnp.float32)
    grad_value_weight = jnp.dot(tokens.T, values_round, preferred_element_type=jnp.float32)
    grad_query_bias = jnp.sum(back_query, axis=0)
    grad_value_bias = jnp.sum(back_values, axis=0)
    back_input = (
        back_first
        + jnp.dot(query_round, query_weight.T, preferred_element_type=jnp.float32)
        + jnp.dot(keys_round, key_weight.T, preferred_element_type=jnp.float32)
        + jnp.dot(values_round, value_weight.T, preferred_element_type=jnp.float32)
    )
    input_grad = jnp.where(live, back_input, cotangent.astype(jnp.float32)).astype(jnp.bfloat16)
    grad_list = [
        grad_query_weight,
        grad_key_weight,
        grad_value_weight,
        grad_output_weight,
        grad_inner_weight,
        grad_outer_weight,
        grad_query_bias,
        grad_value_bias,
        grad_output_bias,
        grad_first_gain,
        grad_first_shift,
        grad_inner_bias,
        grad_outer_bias,
        grad_second_gain,
        grad_second_shift,
    ]
    return (input_grad, grad_list)


def adamw(grad, weights, first, second):
    first_new = 0.9 * first + 0.1 * grad
    second_new = 0.98 * second + 0.02 * grad * grad
    first_hat = first_new / (1.0 - 0.9**STEP)
    second_hat = second_new / (1.0 - 0.98**STEP)
    weights_new = weights - 0.01 * (first_hat / (jnp.sqrt(second_hat) + 1e-06) + 0.01 * weights)
    return (weights_new, first_new, second_new)


def on_device(tokens, cotangent, segment_ids, flat_weights, first_moment, second_moment):
    gathered = lax.all_gather(flat_weights.astype(jnp.bfloat16), "shard", axis=0, tiled=True)
    params = unpack(gathered)
    output, saved = forward_pass(tokens, segment_ids, params)
    input_grad, grads = backward_pass(tokens, cotangent, saved, params)
    local_grad = jnp.concatenate([member.reshape(-1).astype(jnp.bfloat16) for member in grads])
    shards = lax.axis_size("shard")
    owned_len = local_grad.shape[0] // shards
    received = lax.all_to_all(
        local_grad.reshape(shards, owned_len), "shard", split_axis=0, concat_axis=0, tiled=True
    )
    group_part = jnp.sum(received.astype(jnp.float32), axis=0)
    weight_grad = lax.psum(group_part, "rep")
    new_weights, new_first, new_second = adamw(
        weight_grad, flat_weights, first_moment, second_moment
    )
    return (output, input_grad, weight_grad, new_weights, new_first, new_second)


def flip(axis, bit):
    here = lax.axis_index(axis)
    return here + bit * (1 - 2 * (lax.rem(here // bit, 2)))


def own_bit(axis, bit):
    return lax.rem(lax.axis_index(axis) // bit, 2)


LINKS = {
    "core": ("rep", 1),
    "x": ("rep", 2),
    "z1": ("rep", 4),
    "z2": ("rep", 8),
    "y": ("shard", 1),
}


def partner(name):
    axis, bit = LINKS[name]
    return {axis: flip(axis, bit)}


def side(name):
    return own_bit(*LINKS[name])


def greet(names):
    barrier = pltpu.get_barrier_semaphore()
    for name in names:
        pl.semaphore_signal(
            barrier, inc=1, device_id=partner(name), device_id_type=pl.DeviceIdType.MESH
        )
    pl.semaphore_wait(barrier, len(names))


def send(source, target, send_sem, recv_sem, name):
    copy = pltpu.make_async_remote_copy(
        src_ref=source,
        dst_ref=target,
        send_sem=send_sem,
        recv_sem=recv_sem,
        device_id=partner(name),
        device_id_type=pl.DeviceIdType.MESH,
    )
    copy.start()
    return copy


CHUNKS = 6


def gather_kernel(own_ref, full_ref, send_sem, recv_sem):
    owned = own_ref.shape[0]
    chunk = owned // (4 * CHUNKS * 16) * 16
    extra = owned - 4 * CHUNKS * chunk
    mine = side("y")
    other = 1 - mine
    quarter = side("x") * 2 + side("core")
    across = (1 - side("x")) * 2 + side("core")

    def place(part, k):
        return (part * CHUNKS + k) * chunk

    def here(start, size):
        return own_ref.at[pl.ds(pl.multiple_of(start, 16), size)]

    def there(shard, start, size):
        return full_ref.at[pl.ds(pl.multiple_of(shard * owned + start, 16), size)]

    greet(("y", "x", "core"))
    first = []
    for k in range(CHUNKS):
        start = place(quarter, k)
        first.append(
            send(
                here(start, chunk),
                there(mine, start, chunk),
                send_sem.at[0, k],
                recv_sem.at[0, k],
                "y",
            )
        )
    rest = 4 * CHUNKS * chunk
    final = None
    if extra:
        final = send(
            here(rest, extra),
            there(mine, rest, extra),
            send_sem.at[0, CHUNKS],
            recv_sem.at[0, CHUNKS],
            "y",
        )
    step = owned // (16 * 25) * 16 if owned % (16 * 25) == 0 else 16

    def keep(i, carry):
        start = pl.multiple_of(i * step, 16)
        target = pl.multiple_of(mine * owned + i * step, 16)
        full_ref[pl.ds(target, step), :] = own_ref[pl.ds(start, step), :]
        return carry

    lax.fori_loop(0, owned // step, keep, 0)
    second, third, fourth = [], [], []

    def pass_on(part, k, row, name):
        block = there(other, place(part, k), chunk)
        return send(block, block, send_sem.at[row, k], recv_sem.at[row, k], name)

    for k in range(CHUNKS):
        first[k].wait_recv()
        second.append(pass_on(quarter, k, 1, "x"))
        third.append(pass_on(quarter, k, 2, "core"))
        if k > 0:
            second[k - 1].wait_recv()
            fourth.append(pass_on(across, k - 1, 3, "core"))
    last = CHUNKS - 1
    second[last].wait_recv()
    fourth.append(pass_on(across, last, 3, "core"))
    for k in range(CHUNKS):
        third[k].wait_recv()
        fourth[k].wait_recv()
        first[k].wait_send()
        second[k].wait_send()
        third[k].wait_send()
        fourth[k].wait_send()
    if extra:
        final.wait()


def gather_params(own):
    return pl.pallas_call(
        gather_kernel,
        out_shape=jax.ShapeDtypeStruct((2 * own.shape[0], 128), jnp.bfloat16),
        in_specs=[pl.BlockSpec(memory_space=pltpu.VMEM)],
        out_specs=pl.BlockSpec(memory_space=pltpu.VMEM),
        scratch_shapes=[
            pltpu.SemaphoreType.DMA((4, CHUNKS + 1)),
            pltpu.SemaphoreType.DMA((4, CHUNKS + 1)),
        ],
        compiler_params=pltpu.CompilerParams(
            collective_id=0, has_side_effects=True, vmem_limit_bytes=56 * 2**20
        ),
        name="gather_params",
    )(own)


PLACE = (("x", "z1", "z2"), ("x", "z1", "z2"), ("z1", "x", "z2"))
ORDER = (("y", "x", "z1", "z2"), ("x", "z1", "y", "z2"), ("z1", "y", "x", "z2"))
SUM_LINKS = ("core", "y", "x", "z1", "z2")


def index_of(done, part, name=None, swap=False):
    entries = []
    for dim in ("y",) + PLACE[part]:
        if dim == name:
            entries.append(1 - side(dim) if swap else side(dim))
        elif dim in done:
            entries.append(side(dim))
        else:
            entries.append(slice(None))
    return tuple(entries)


def add_blocks(shape, store, other):
    total = math.prod(shape)

    def body(i, carry):
        index = []
        rest = i
        for extent in reversed(shape):
            index.append(lax.rem(rest, extent))
            rest = rest // extent
        index = tuple(reversed(index))
        here = store.at[index]
        there = other.at[index]
        here[...] = (here[...].astype(jnp.float32) + there[...].astype(jnp.float32)).astype(
            jnp.bfloat16
        )
        return carry

    lax.fori_loop(0, total, body, 0)


def reduce_kernel(grad_ref, tail_ref, out_ref, total_ref, own, tail_sum, tail_in, *rest):
    steps = len(ORDER[0])
    landing = [rest[0:3]] + [rest[3 + 3 * t : 6 + 3 * t] for t in range(steps)]
    send_sem, recv_sem, local_sem, tail_send, tail_recv = rest[3 + 3 * steps :]

    def tail_step(step):
        copy = send(
            tail_sum.at[step],
            tail_in.at[step],
            tail_send.at[step],
            tail_recv.at[step],
            SUM_LINKS[step],
        )
        started.append(copy)
        return copy

    core = side("core")
    greet(SUM_LINKS)
    copies, local = [], []
    for part in range(3):
        copies.append(
            send(
                grad_ref.at[:, part, 1 - core],
                landing[0][part],
                send_sem.at[0, part],
                recv_sem.at[0, part],
                "core",
            )
        )
        own_copy = pltpu.make_async_copy(
            grad_ref.at[:, part, core], own.at[part], local_sem.at[part]
        )
        own_copy.start()
        local.append(own_copy)
    started = list(copies)
    tail_sum[0] = tail_ref[...]
    tail_copy = tail_step(0)
    done = [(), (), ()]
    for step in range(steps + 1):
        for part in range(3):
            copies[part].wait_recv()
            if step == 0:
                local[part].wait()
                store = own.at[part]
            else:
                name = ORDER[part][step - 1]
                store = own.at[(part,) + index_of(done[part], part, name)]
                done[part] = done[part] + (name,)
            source = landing[step][part]
            lead = source.shape[:-2]
            add_blocks(lead, store, source)
            if step < steps:
                name = ORDER[part][step]
                copies[part] = send(
                    own.at[(part,) + index_of(done[part], part, name, True)],
                    landing[step + 1][part],
                    send_sem.at[step + 1, part],
                    recv_sem.at[step + 1, part],
                    name,
                )
                started.append(copies[part])
            else:
                out_ref[part] = own[(part,) + index_of(done[part], part)]
        tail_copy.wait_recv()
        if step < steps:
            tail_sum[step + 1] = tail_sum[step] + tail_in[step]
            tail_copy = tail_step(step + 1)
        else:
            total_ref[...] = tail_sum[step] + tail_in[step]
    for copy in started:
        copy.wait_send()


def reduce_scatter(rows, tail):
    piece, width = rows.shape[0] // 96, rows.shape[1]
    scratch = [pltpu.VMEM((3, 2, 2, 2, 2, piece, width), jnp.bfloat16)]
    scratch += [pltpu.VMEM((5,) + tail.shape, jnp.float32)] * 2
    scratch += [pltpu.VMEM((2, 2, 2, 2, piece, width), jnp.bfloat16)] * 3
    for step in range(4):
        for part in range(3):
            used = ORDER[part][: step + 1]
            lead = tuple(2 for dim in ("y",) + PLACE[part] if dim not in used)
            scratch.append(pltpu.VMEM(lead + (piece, width), jnp.bfloat16))
    scratch += [
        pltpu.SemaphoreType.DMA((5, 3)),
        pltpu.SemaphoreType.DMA((5, 3)),
        pltpu.SemaphoreType.DMA((3,)),
        pltpu.SemaphoreType.DMA((5,)),
        pltpu.SemaphoreType.DMA((5,)),
    ]
    return pl.pallas_call(
        reduce_kernel,
        out_shape=(
            jax.ShapeDtypeStruct((3, piece, width), jnp.bfloat16),
            jax.ShapeDtypeStruct(tail.shape, jnp.float32),
        ),
        in_specs=[
            pl.BlockSpec(memory_space=pl.ANY),
            pl.BlockSpec(memory_space=pltpu.VMEM),
        ],
        out_specs=(
            pl.BlockSpec(memory_space=pltpu.VMEM),
            pl.BlockSpec(memory_space=pltpu.VMEM),
        ),
        scratch_shapes=scratch,
        compiler_params=pltpu.CompilerParams(
            collective_id=1, has_side_effects=True, vmem_limit_bytes=56 * 2**20
        ),
        name="reduce_scatter",
    )(rows.reshape(2, 3, 2, 2, 2, 2, piece, width), tail)


SPREAD = (("z2", "z1", "x", "core"), ("z2", "x", "z1", "core"), ("x", "z2", "z1", "core"))


def spread_kernel(piece_ref, full_ref, send_sem, recv_sem):
    def index(part, done):
        return (part,) + tuple(
            slice(None) if dim in done else side(dim) for dim in ("core",) + PLACE[part]
        )

    greet(("core", "x", "z1", "z2"))
    copies, started = [], []
    for part in range(3):
        full_ref[index(part, ())] = piece_ref[part]
    for step in range(4):
        for part in range(3):
            if step > 0:
                copies[part].wait_recv()
            block = full_ref.at[index(part, SPREAD[part][:step])]
            copy = send(
                block,
                block,
                send_sem.at[step, part],
                recv_sem.at[step, part],
                SPREAD[part][step],
            )
            started.append(copy)
            if step > 0:
                copies[part] = copy
            else:
                copies.append(copy)
    for part in range(3):
        copies[part].wait_recv()
    for copy in started:
        copy.wait_send()


def spread(pieces):
    rows = pieces.shape[1]
    full = pl.pallas_call(
        spread_kernel,
        out_shape=jax.ShapeDtypeStruct((3, 2, 2, 2, 2, rows, 128), jnp.bfloat16),
        in_specs=[pl.BlockSpec(memory_space=pltpu.VMEM)],
        out_specs=pl.BlockSpec(memory_space=pltpu.VMEM),
        scratch_shapes=[
            pltpu.SemaphoreType.DMA((4, 3)),
            pltpu.SemaphoreType.DMA((4, 3)),
        ],
        compiler_params=pltpu.CompilerParams(
            collective_id=2, has_side_effects=True, vmem_limit_bytes=40 * 2**20
        ),
        name="spread",
    )(pieces)
    return full.reshape(3 * 16 * rows, 128)


def on_device_pair(tokens, cotangent, segment_ids, flat_weights, first_moment, second_moment):
    owned = flat_weights.shape[0]
    full = gather_params(flat_weights.reshape(owned // 128, 128).astype(jnp.bfloat16))
    params = unpack(full.reshape(-1))
    output, saved = forward_pass(tokens, segment_ids, params)
    input_grad, grads = backward_pass(tokens, cotangent, saved, params)
    rounded = [member.astype(jnp.bfloat16) for member in grads]
    rows = jnp.concatenate([member.reshape(-1, D) for member in rounded[:6]])
    half = rows.shape[0] // 2
    vectors = jnp.concatenate(rounded[6:])
    over = owned - half * D
    tail = jnp.concatenate([rows[half : half + over // D].reshape(-1), vectors])
    pieces, tail = reduce_scatter(rows, tail.astype(jnp.float32).reshape(-1, 128))
    tail = tail.reshape(-1)
    main = spread(pieces.reshape(3, -1, 128))
    first_shard = lax.axis_index("shard") == 0
    fill = jnp.zeros((vectors.shape[0] - over,), jnp.float32)
    tail = jnp.where(first_shard, jnp.concatenate([tail[:over], fill]), tail[over:])
    joined = jnp.concatenate([main, tail.astype(jnp.bfloat16).reshape(-1, 128)])
    start = jnp.where(first_shard, 0, over // 128)
    weight_grad = lax.dynamic_slice_in_dim(joined, start, owned // 128).astype(jnp.float32)
    weight_grad = weight_grad.reshape(owned)
    new_weights, new_first, new_second = adamw(
        weight_grad, flat_weights, first_moment, second_moment
    )
    return (output, input_grad, weight_grad, new_weights, new_first, new_second)


def solution(mesh):
    paired = mesh.shape["shard"] == 2 and mesh.shape["rep"] == 16
    return jax.shard_map(
        on_device_pair if paired else on_device,
        mesh=mesh,
        in_specs=(
            P(("rep", "shard"), None),
            P(("rep", "shard"), None),
            P(("rep", "shard")),
            P("shard"),
            P("shard"),
            P("shard"),
        ),
        out_specs=(
            P(("rep", "shard"), None),
            P(("rep", "shard"), None),
            P("shard"),
            P("shard"),
            P("shard"),
            P("shard"),
        ),
        check_vma=False,
    )
```
